512 devices in a mesh: grp: 32 (over y, x_hi, core), frq: 16 (over z, x_lo).
Axes of the slice: x: 4 (x_hi: 2, x_lo: 2; x = x_hi * 2 + x_lo), y: 8, z: 8, core: 2. Of those that a mesh axis runs over, the one named last changes fastest.
Arguments:
- spectra: bfloat16 [32, 512, 240, 128], P('grp', 'frq'), may hold values from -6 to 6
- band_weight: float32 [512], replicated, may hold values from 0.25 to 4
Outputs:
- correlations: bfloat16 [2, 32, 4096, 1024], P(None, 'grp', 'frq')
The draws below stay inside these ranges and needn't reach their ends.
All inputs are finite; a program needn't handle non-finite values.
Results may differ from the reference program's by a relative error of at most 0.0058.
Values may be sent and summed in bfloat16 or wider, within the bound.
A program may use at most 64 MiB of HBM per device.

```python
import math
import jax
import jax.numpy as jnp
from jax import lax

STA = 64
FREQS = 512
WIN = 240
ROUNDS = 2
GROUPS = 32


def steps_of(own_key, dims, pieces, least, high):
    factor_of = 1.0
    for axis_at, shards_of in pieces:
        heights = jax.random.uniform(jax.random.fold_in(jax.random.fold_in(own_key, 6), axis_at), (shards_of,), jnp.float32, least / len(pieces), high / len(pieces))
        factor_of = factor_of * jnp.repeat(jnp.exp(heights), dims[axis_at] // shards_of).reshape((-1,) + (1,) * (len(dims) - 1 - axis_at))
    return factor_of


def bell_draw(key, extent, width, reach, cuts=(), kind=jnp.bfloat16):
    level = steps_of(key, extent, cuts, -0.22, 0.18) if cuts else 1.0
    array = jax.random.normal(key, extent, jnp.float32) * width * level
    return jnp.minimum(jnp.maximum(array, -reach), reach).astype(kind)


def setup_inputs(seed: int = 0) -> dict:
    arg_keys = jax.random.split(jax.random.key(seed), 3)
    spectra = bell_draw(arg_keys[0], (GROUPS, FREQS, WIN, 2 * STA), 1.0, 6.0, ((0, 32), (1, 16)))
    band_weight = jnp.clip(jnp.exp(jax.random.uniform(arg_keys[1], (FREQS,), jnp.float32, math.log(0.25), math.log(4.0))), 0.25, 4.0)
    return {"spectra": spectra, "band_weight": band_weight}


def inverse_table(band_weight):
    bin_count = band_weight.shape[0]
    lag_count = 2 * bin_count
    phase_index = jnp.arange(bin_count, dtype=jnp.int32)[:, None] * jnp.arange(lag_count, dtype=jnp.int32)[None, :] % lag_count
    phase_angle = phase_index.astype(jnp.float32) * (2.0 * math.pi / lag_count)
    weighting = band_weight[:, None] * (1.0 / math.sqrt(bin_count))
    return jnp.stack([weighting * jnp.cos(phase_angle), -weighting * jnp.sin(phase_angle)], 1).astype(jnp.bfloat16)

def cross_stack(local_block, partner_block):
    windows = local_block.shape[1]
    half_width = local_block.shape[2] // 2
    product = jnp.einsum('fwa,fwb->fab', local_block.astype(jnp.float32), partner_block.astype(jnp.float32))
    real_part = product[:, :half_width, :half_width] + product[:, half_width:, half_width:]
    imag_part = product[:, half_width:, :half_width] - product[:, :half_width, half_width:]
    scaled = jnp.stack([real_part, imag_part], 1) * (1.0 / math.sqrt(windows))
    return scaled.reshape(scaled.shape[0], 2, half_width * half_width).astype(jnp.bfloat16)

def reference(spectra, band_weight):
    lag_table = inverse_table(band_weight).astype(jnp.float32)
    group_count = spectra.shape[0]
    outputs = []
    for turn_index in range(ROUNDS):
        offset = turn_index + 1

        def one_group(group_id):
            local_block = lax.dynamic_index_in_dim(spectra, group_id, 0, keepdims=False)
            partner_id = ((group_id - offset) % group_count).astype(jnp.int32)
            partner_block = lax.dynamic_index_in_dim(spectra, partner_id, 0, keepdims=False)
            stacked = cross_stack(local_block, partner_block)
            lagged = jnp.einsum('fcp,fcl->pl', stacked.astype(jnp.float32), lag_table)
            return lagged.astype(jnp.bfloat16)
        outputs.append(lax.map(one_group, jnp.arange(group_count, dtype=jnp.int32)))
    return jnp.stack(outputs)
```

```python
import functools
import math

import jax
import jax.numpy as jnp
from jax import lax
from jax.experimental import pallas as pl
from jax.experimental.pallas import tpu as pltpu
from jax.sharding import PartitionSpec as P

ROUNDS = 2
CHUNKS = 2
PIECES = 2
RUN = 4
LANES = 128
MESH = pl.DeviceIdType.MESH
F32 = jnp.float32
BF16 = jnp.bfloat16


def stack_kernel(
    rows_y, rows_z, spectra, weight, out, held, table, weights, work, packed, relay, landed, sorted_, total,
    x_send, x_recv, y_send, y_recv, z_send, z_recv, row_send, row_recv,
):
    grp, frq = lax.axis_index("grp"), lax.axis_index("frq")
    y, xh, core = grp // 4, (grp // 2) % 2, grp % 2
    z, xl = frq // 2, frq % 2

    def device(y_, xh_, core_, z_, xl_):
        return (y_ * 4 + xh_ * 2 + core_, z_ * 2 + xl_)

    up, down = (y + 1) % rows_y, (y + rows_y - 1) % rows_y
    row = [(e, a, b) for e in range(2) for a in range(2) for b in range(2)]

    def in_row(e, a, b):
        return device(y, (xh + e) % 2, (core + b) % 2, z, (xl + a) % 2)

    barrier = pltpu.get_barrier_semaphore()
    partners = [in_row(*rel) for rel in row[1:]]
    partners += [device(y, xh, core, (z + k) % rows_z, xl) for k in range(1, rows_z)]
    partners += [device(up, xh, core, z, xl), device(down, xh, core, z, xl)]
    for partner in partners:
        pl.semaphore_signal(barrier, inc=1, device_id=partner, device_id_type=MESH)
    pl.semaphore_wait(barrier, len(partners))

    part = RUN // PIECES
    x_copies = []
    for n in range(CHUNKS):
        for p in range(PIECES):
            for e in range(2):
                for b in range(2):
                    to_xh, to_core = (xh + e) % 2, (core + b) % 2
                    first = n * 4 * RUN + RUN * (2 * to_xh + to_core) + part * p
                    copy = pltpu.make_async_remote_copy(
                        src_ref=spectra.at[0, pl.ds(first, part)],
                        dst_ref=held.at[2 + 2 * xh + core, pl.ds(n * RUN + part * p, part)],
                        send_sem=x_send.at[n, p, 2 * e + b],
                        recv_sem=x_recv.at[n, p, 2 * e + b],
                        device_id=device(y, to_xh, to_core, z, 1 - xl),
                        device_id_type=MESH,
                    )
                    copy.start()
                    x_copies.append(copy)

    def wait_x(n, p):
        for e in range(2):
            for b in range(2):
                slot = 2 + 2 * ((xh + e) % 2) + (core + b) % 2
                here = held.at[slot, pl.ds(n * RUN + part * p, part)]
                pltpu.make_async_copy(here, here, x_recv.at[n, p, 2 * e + b]).wait()

    def y_copy(n, p):
        return pltpu.make_async_remote_copy(
            src_ref=held.at[pl.ds(4, 2), pl.ds(n * RUN + part * p, part)],
            dst_ref=held.at[pl.ds(0, 2), pl.ds(n * RUN + part * p, part)],
            send_sem=y_send.at[n, p],
            recv_sem=y_recv.at[n, p],
            device_id=device(up, xh, core, z, xl),
            device_id_type=MESH,
        )

    def forward(n):
        for p in range(PIECES):
            wait_x(n, p)
            y_copy(n, p).start()

    lags = table.shape[2]
    bins = lags // 2
    for b in range(bins // LANES):
        wide = jnp.broadcast_to(weight[b : b + 1, :], (LANES, LANES))
        weights[pl.ds(b * LANES, LANES), :] = wide.T * (1.0 / math.sqrt(bins))

    group_rows = lax.broadcasted_iota(jnp.int32, (8, LANES), 0)
    group_cols = lax.broadcasted_iota(jnp.int32, (8, LANES), 1)
    turn = 2.0 * math.pi / lags
    steps = []
    for s in range(lags // LANES):
        angle = ((group_rows * (s * LANES)) % lags).astype(F32) * turn
        steps.append((jnp.cos(angle), jnp.sin(angle)))

    def table_rows(index, carry):
        n, group = index // (4 * rows_z), index % (4 * rows_z)
        hi, lo, depth = group // (2 * rows_z), (group // rows_z) % 2, group % rows_z
        first = pl.multiple_of(depth * 64 + (1 - lo) * 32 + n * 16 + hi * 8, 8)
        angle = (((group_rows + first) * group_cols) % lags).astype(F32) * turn
        scale = weights[pl.ds(first, 8), :]
        base_cos, base_sin = jnp.cos(angle) * scale, jnp.sin(angle) * scale
        at = pl.multiple_of(group * 16, 16)
        for s, (step_cos, step_sin) in enumerate(steps):
            real = base_cos * step_cos - base_sin * step_sin
            imag = base_sin * step_cos + base_cos * step_sin
            table[n, pl.ds(at, 16), s * LANES : (s + 1) * LANES] = jnp.concatenate([real, -imag], 0).astype(BF16)
        return carry

    lax.fori_loop(0, CHUNKS * 4 * rows_z, table_rows, 0)

    windows, width = held.shape[2], held.shape[3]
    half = width // 2
    tiles = packed.shape[5] // LANES
    lane = lax.broadcasted_iota(jnp.int32, (8, LANES), 1)
    sign = jnp.where(lax.broadcasted_iota(jnp.int32, (half, width), 1) < half, 1.0, -1.0)

    def products(n, m, c_to):
        hi = m // 2

        def one(f, carry):
            at = n * RUN + f
            pair = jnp.concatenate([held[m + 1, at], held[m, at]], 1)
            product = lax.dot_general(
                held[m + 2, at], pair, (((0,), (0,)), ((), ())), preferred_element_type=F32
            ) * (1.0 / math.sqrt(windows))
            for r in range(ROUNDS):
                block = product[:, r * width : (r + 1) * width]
                both = block[:half] * sign + pltpu.roll(block[half:], half, 1)
                work[pl.ds(pl.multiple_of((r * RUN + f) * half, half), half), :] = both
            return carry

        lax.fori_loop(0, RUN, one, 0, unroll=True)
        for pair in range(half // 2):
            first = work[pl.ds(2 * pair, 8, stride=half), :]
            second = work[pl.ds(2 * pair + 1, 8, stride=half), :]
            real = jnp.where(lane < half, first, pltpu.roll(second, half, 1))
            imag = jnp.where(lane < half, pltpu.roll(first, half, 1), second)
            depth, rest = pair // (2 * tiles), pair % (2 * tiles)
            lo, tile = rest // tiles, rest % tiles
            packed[2 * n + hi, depth, c_to, lo, :, tile * LANES : (tile + 1) * LANES] = jnp.concatenate(
                [real, imag], 0
            ).astype(BF16)

    def wave(n, hi):
        for c_to in range(2):
            products(n, 2 * hi + c_to, c_to)

    def z_copy(n, hi, k):
        w = 2 * n + hi
        return pltpu.make_async_remote_copy(
            src_ref=packed.at[w, (z + k) % rows_z],
            dst_ref=relay.at[w, z],
            send_sem=z_send.at[w, k],
            recv_sem=z_recv.at[w, k],
            device_id=device(y, xh, core, (z + k) % rows_z, xl),
            device_id_type=MESH,
        )

    def own_copy(n, hi):
        w = 2 * n + hi
        return pltpu.make_async_copy(packed.at[w, z], relay.at[w, z], z_recv.at[w, 0])

    def send_z(n, hi):
        for k in range(1, rows_z):
            z_copy(n, hi, k).start()
        own_copy(n, hi).start()

    def wait_z(n, hi):
        w = 2 * n + hi
        for k in range(rows_z):
            here = relay.at[w, (z + rows_z - k) % rows_z]
            pltpu.make_async_copy(here, here, z_recv.at[w, k]).wait()

    def row_copy(n, hi, e, a, b):
        w = 2 * n + hi
        return pltpu.make_async_remote_copy(
            src_ref=relay.at[w, :, (core + b) % 2, (xl + a) % 2],
            dst_ref=landed.at[n, 4 * xh + 2 * xl + core],
            send_sem=row_send.at[n, 4 * e + 2 * a + b],
            recv_sem=row_recv.at[n, 4 * e + 2 * a + b],
            device_id=device(y, hi, (core + b) % 2, z, (xl + a) % 2),
            device_id_type=MESH,
        )

    def send_row(n, hi):
        for e in range(2):
            @pl.when((xh + e) % 2 == hi)
            def _():
                for a in range(2):
                    for b in range(2):
                        if (e, a, b) == (0, 0, 0):
                            pltpu.make_async_copy(
                                relay.at[2 * n + hi, :, core, xl],
                                landed.at[n, 4 * xh + 2 * xl + core],
                                row_recv.at[n, 0],
                            ).start()
                        else:
                            row_copy(n, hi, e, a, b).start()

    def wait_row(n):
        for k, (e, a, b) in enumerate(row):
            here = landed.at[n, 4 * ((xh + e) % 2) + 2 * ((xl + a) % 2) + (core + b) % 2]
            pltpu.make_async_copy(here, here, row_recv.at[n, k]).wait()

    pairs = landed.shape[4]
    upper = lax.broadcasted_iota(jnp.int32, (8, pairs), 0) < RUN

    def sort(n):
        def one(group, carry):
            source, depth = group // rows_z, group % rows_z
            first = landed[n, 2 * source, depth].astype(F32)
            second = landed[n, 2 * source + 1, depth].astype(F32)
            kept, moved = [], []
            for c in range(2):
                a, b = first[8 * c : 8 * c + 8], second[8 * c : 8 * c + 8]
                kept.append(jnp.where(upper, a, pltpu.roll(b, RUN, 0)))
                moved.append(jnp.where(upper, pltpu.roll(a, RUN, 0), b))
            at = pl.multiple_of(group * 16, 16)
            sorted_[n, 0, pl.ds(at, 16), :] = jnp.concatenate(kept, 0).astype(BF16)
            sorted_[n, 1, pl.ds(at, 16), :] = jnp.concatenate(moved, 0).astype(BF16)
            return carry

        lax.fori_loop(0, 4 * rows_z, one, 0)

    def lag_product(n):
        step = min(256, lags)

        def one(index, carry):
            r, at = index // (lags // step), pl.multiple_of(index % (lags // step) * step, step)
            value = lax.dot_general(
                sorted_[n, r], table[n, :, pl.ds(at, step)], (((0,), (0,)), ((), ())), preferred_element_type=F32
            )
            if n == 0:
                total[r, :, pl.ds(at, step)] = value
            else:
                out[r, 0, :, pl.ds(at, step)] = (total[r, :, pl.ds(at, step)] + value).astype(BF16)
            return carry

        lax.fori_loop(0, ROUNDS * (lags // step), one, 0)

    def wait_y(n):
        for p in range(PIECES):
            y_copy(n, p).wait_recv()

    forward(0)
    wave(0, 1)
    send_z(0, 1)
    wait_y(0)
    wave(0, 0)
    send_z(0, 0)
    forward(1)
    wave(1, 1)
    send_z(1, 1)
    wait_z(0, 1)
    send_row(0, 1)
    wait_z(0, 0)
    send_row(0, 0)
    wait_y(1)
    wave(1, 0)
    send_z(1, 0)
    wait_z(1, 1)
    send_row(1, 1)
    wait_row(0)
    sort(0)
    lag_product(0)
    wait_z(1, 0)
    send_row(1, 0)
    wait_row(1)
    sort(1)
    lag_product(1)

    for copy in x_copies:
        copy.wait_send()
    for n in range(CHUNKS):
        for p in range(PIECES):
            y_copy(n, p).wait_send()
        for hi in range(2):
            for k in range(1, rows_z):
                z_copy(n, hi, k).wait_send()
            for e in range(2):
                @pl.when((xh + e) % 2 == hi)
                def _():
                    for a in range(2):
                        for b in range(2):
                            if (e, a, b) != (0, 0, 0):
                                row_copy(n, hi, e, a, b).wait_send()


def local(rows_y, rows_z, spectra, band_weight):
    _, freqs, windows, width = spectra.shape
    bins = band_weight.shape[0]
    lags = 2 * bins
    pairs = (width // 2) ** 2 // (2 * rows_z)
    held_freqs = CHUNKS * RUN
    rows = 4 * rows_z * 16
    dma = pltpu.SemaphoreType.DMA
    return pl.pallas_call(
        functools.partial(stack_kernel, rows_y, rows_z),
        name="stack",
        out_shape=jax.ShapeDtypeStruct((ROUNDS, 1, pairs, lags), BF16),
        in_specs=[pl.BlockSpec(memory_space=pl.ANY), pl.BlockSpec(memory_space=pltpu.VMEM)],
        out_specs=pl.BlockSpec(memory_space=pltpu.VMEM),
        scratch_shapes=[
            pltpu.VMEM((6, held_freqs, windows, width), BF16),
            pltpu.VMEM((CHUNKS, rows, lags), BF16),
            pltpu.VMEM((bins, LANES), F32),
            pltpu.VMEM((ROUNDS * RUN * width // 2, width), F32),
            pltpu.VMEM((2 * CHUNKS, rows_z, 2, 2, 16, pairs), BF16),
            pltpu.VMEM((2 * CHUNKS, rows_z, 2, 2, 16, pairs), BF16),
            pltpu.VMEM((CHUNKS, 8, rows_z, 16, pairs), BF16),
            pltpu.VMEM((CHUNKS, ROUNDS, rows, pairs), BF16),
            pltpu.VMEM((ROUNDS, pairs, lags), F32),
            dma((CHUNKS, PIECES, 4)),
            dma((CHUNKS, PIECES, 4)),
            dma((CHUNKS, PIECES)),
            dma((CHUNKS, PIECES)),
            dma((2 * CHUNKS, rows_z)),
            dma((2 * CHUNKS, rows_z)),
            dma((CHUNKS, 8)),
            dma((CHUNKS, 8)),
        ],
        compiler_params=pltpu.CompilerParams(
            collective_id=0, has_side_effects=True, vmem_limit_bytes=40 * 2**20
        ),
    )(spectra, band_weight.reshape(bins // LANES, LANES))


def solution(mesh):
    rows_y, rows_z = mesh.shape["grp"] // 4, mesh.shape["frq"] // 2
    return jax.shard_map(
        functools.partial(local, rows_y, rows_z),
        mesh=mesh,
        in_specs=(P("grp", "frq", None, None), P()),
        out_specs=P(None, "grp", "frq", None),
        check_vma=False,
    )
```

```python
import functools
import math

import jax
import jax.numpy as jnp
from jax import lax
from jax.experimental import pallas as pl
from jax.experimental.pallas import tpu as pltpu
from jax.sharding import PartitionSpec as P

ROUNDS = 2
CHUNKS = 4
RUN = 2
LANES = 128
MESH = pl.DeviceIdType.MESH
F32 = jnp.float32
BF16 = jnp.bfloat16


def stack_kernel(
    rows_y, rows_z, spectra, weight_in, out, weight, held, table, weights, work, packed, relay, landed, sorted_, total,
    x_send, x_recv, y_send, y_recv, z_send, z_recv, row_send, row_recv, direct_send, direct_recv, own_sem,
):
    grp, frq = lax.axis_index("grp"), lax.axis_index("frq")
    y, xh, core = grp // 4, (grp // 2) % 2, grp % 2
    z, xl = frq // 2, frq % 2

    def device(y_, xh_, core_, z_, xl_):
        return (y_ * 4 + xh_ * 2 + core_, z_ * 2 + xl_)

    up, down = (y + 1) % rows_y, (y + rows_y - 1) % rows_y
    row = [(e, a, b) for e in range(2) for a in range(2) for b in range(2)]

    def in_plane(k, e, a, b):
        return device(y, (xh + e) % 2, (core + b) % 2, (z + k) % rows_z, (xl + a) % 2)

    windows, width = held.shape[2], held.shape[3]
    whole, halves = [(0, windows)], [(0, LANES), (LANES, windows - LANES)]
    pieces = [
        [(n * RUN + f, *cut) for f in range(RUN) for cut in (halves if n == CHUNKS - 1 else whole)]
        for n in range(CHUNKS)
    ]

    barrier = pltpu.get_barrier_semaphore()
    plane = [(k, *rel) for k in range(rows_z) for rel in row]
    partners = [in_plane(*rel) for rel in plane[1:]]
    partners += [device(up, xh, core, z, xl), device(down, xh, core, z, xl)]
    for partner in partners:
        pl.semaphore_signal(barrier, inc=1, device_id=partner, device_id_type=MESH)
    pl.semaphore_wait(barrier, len(partners))

    weight_copy = pltpu.make_async_copy(weight_in, weight, own_sem)
    weight_copy.start()

    x_copies = []
    for n in range(CHUNKS):
        for p, (f, row_first, row_count) in enumerate(pieces[n]):
            for e in range(2):
                for b in range(2):
                    to_xh, to_core = (xh + e) % 2, (core + b) % 2
                    source = n * 3 * RUN + RUN * (2 * to_xh + to_core) + f
                    copy = pltpu.make_async_remote_copy(
                        src_ref=spectra.at[0, source, pl.ds(row_first, row_count)],
                        dst_ref=held.at[2 + 2 * xh + core, f, pl.ds(row_first, row_count)],
                        send_sem=x_send.at[n, p, 2 * e + b],
                        recv_sem=x_recv.at[n, p, 2 * e + b],
                        device_id=device(y, to_xh, to_core, z, 1 - xl),
                        device_id_type=MESH,
                    )
                    copy.start()
                    x_copies.append(copy)

    def wait_x(n, p):
        f, row_first, row_count = pieces[n][p]
        for e in range(2):
            for b in range(2):
                slot = 2 + 2 * ((xh + e) % 2) + (core + b) % 2
                here = held.at[slot, f, pl.ds(row_first, row_count)]
                pltpu.make_async_copy(here, here, x_recv.at[n, p, 2 * e + b]).wait()

    def y_copy(n, p):
        f, row_first, row_count = pieces[n][p]
        return pltpu.make_async_remote_copy(
            src_ref=held.at[pl.ds(4, 2), f, pl.ds(row_first, row_count)],
            dst_ref=held.at[pl.ds(0, 2), f, pl.ds(row_first, row_count)],
            send_sem=y_send.at[n, p],
            recv_sem=y_recv.at[n, p],
            device_id=device(up, xh, core, z, xl),
            device_id_type=MESH,
        )

    def forward(n, p):
        wait_x(n, p)
        y_copy(n, p).start()

    lags = table.shape[1]
    bins = lags // 2
    weight_copy.wait()
    for b in range(bins // LANES):
        wide = jnp.broadcast_to(weight[b : b + 1, :], (LANES, LANES))
        weights[pl.ds(b * LANES, LANES), :] = wide.T * (1.0 / math.sqrt(bins))

    group_rows = lax.broadcasted_iota(jnp.int32, (8, LANES), 0)
    group_cols = lax.broadcasted_iota(jnp.int32, (8, LANES), 1)
    turn = 2.0 * math.pi / lags
    steps = []
    for s in range(lags // LANES):
        angle = ((group_rows * (s * LANES)) % lags).astype(F32) * turn
        steps.append((jnp.cos(angle), jnp.sin(angle)))

    def table_rows(index, carry):
        n, group = index // (2 * rows_z), index % (2 * rows_z)
        lo, depth = group // rows_z, group % rows_z
        first = pl.multiple_of(depth * 64 + (1 - lo) * 32 + n * 8, 8)
        angle = (((group_rows + first) * group_cols) % lags).astype(F32) * turn
        scale = weights[pl.ds(first, 8), :]
        base_cos, base_sin = jnp.cos(angle) * scale, jnp.sin(angle) * scale
        at = pl.multiple_of(index * 16, 16)
        for s, (step_cos, step_sin) in enumerate(steps):
            real = base_cos * step_cos - base_sin * step_sin
            imag = base_sin * step_cos + base_cos * step_sin
            table[pl.ds(at, 16), s * LANES : (s + 1) * LANES] = jnp.concatenate([real, -imag], 0).astype(BF16)
        return carry

    lax.fori_loop(0, CHUNKS * 2 * rows_z, table_rows, 0)

    half = width // 2
    lane = lax.broadcasted_iota(jnp.int32, (8, LANES), 1) < half
    sublane = lax.broadcasted_iota(jnp.int32, (8, LANES), 0)
    sign = jnp.where(lax.broadcasted_iota(jnp.int32, (half, width), 1) < half, 1.0, -1.0)

    def products(n, hi):
        for c_to in range(2):
            m = 2 * hi + c_to
            for f in range(RUN):
                at = n * RUN + f
                pair = jnp.concatenate([held[m + 1, at], held[m, at]], 1)
                product = lax.dot_general(
                    held[m + 2, at], pair, (((0,), (0,)), ((), ())), preferred_element_type=F32
                ) * (1.0 / math.sqrt(windows))
                for r in range(ROUNDS):
                    block = product[:, r * width : (r + 1) * width]
                    both = block[:half] * sign + pltpu.roll(block[half:], half, 1)
                    work[pl.ds(((c_to * ROUNDS + r) * RUN + f) * half, half), :] = both
        for shard in range(half // 4):
            real, imag = [], []
            for h in range(2):
                first = work[pl.ds(4 * shard + 2 * h, 8, stride=half), :]
                second = work[pl.ds(4 * shard + 2 * h + 1, 8, stride=half), :]
                real.append(jnp.where(lane, first, pltpu.roll(second, half, 1)))
                imag.append(jnp.where(lane, pltpu.roll(first, half, 1), second))
            for c_to in range(2):
                parts = []
                for lower, upper in (real, imag):
                    if c_to:
                        lower = pltpu.roll(lower, 4, 0)
                    else:
                        upper = pltpu.roll(upper, 4, 0)
                    parts.append(jnp.where(sublane < 4, lower, upper))
                packed[2 * n + hi, shard // 2, c_to, shard % 2] = jnp.concatenate(parts, 0).astype(BF16)

    last = CHUNKS - 1
    far_first = sorted(range(1, rows_z), key=lambda k: -min(k, rows_z - k))

    def z_copy(n, hi, k):
        w = 2 * n + hi
        return pltpu.make_async_remote_copy(
            src_ref=packed.at[w, (z + k) % rows_z],
            dst_ref=relay.at[w, z],
            send_sem=z_send.at[w, k],
            recv_sem=z_recv.at[w, k],
            device_id=device(y, xh, core, (z + k) % rows_z, xl),
            device_id_type=MESH,
        )

    def wave(n, hi):
        products(n, hi)
        for k in far_first:
            z_copy(n, hi, k).start()
        w = 2 * n + hi
        pltpu.make_async_copy(packed.at[w, z], relay.at[w, z], z_recv.at[w, 0]).start()

    def wait_z(n, hi):
        w = 2 * n + hi
        for k in range(rows_z):
            here = relay.at[w, (z + rows_z - k) % rows_z]
            pltpu.make_async_copy(here, here, z_recv.at[w, k]).wait()

    own_source = 4 * xh + 2 * xl + core

    def row_copy(n, hi, a, b):
        return pltpu.make_async_remote_copy(
            src_ref=relay.at[2 * n + hi, :, (core + b) % 2, (xl + a) % 2],
            dst_ref=landed.at[n, own_source],
            send_sem=row_send.at[n, hi, 2 * a + b],
            recv_sem=row_recv.at[n, 4 * ((xh + hi) % 2) + 2 * a + b],
            device_id=device(y, hi, (core + b) % 2, z, (xl + a) % 2),
            device_id_type=MESH,
        )

    def send_row(n, hi):
        wait_z(n, hi)
        for a, b in ((1, 0), (1, 1), (0, 1)):
            row_copy(n, hi, a, b).start()

        @pl.when(xh != hi)
        def _():
            row_copy(n, hi, 0, 0).start()

        @pl.when(xh == hi)
        def _():
            pltpu.make_async_copy(
                relay.at[2 * n + hi, :, core, xl], landed.at[n, own_source], row_recv.at[n, 0]
            ).start()

    def direct_copy(hi, k, a, b):
        to_z, to_core, to_xl = (z + k) % rows_z, (core + b) % 2, (xl + a) % 2
        return pltpu.make_async_remote_copy(
            src_ref=packed.at[2 * last + hi, to_z, to_core, to_xl],
            dst_ref=landed.at[last, own_source, z],
            send_sem=direct_send.at[hi, k, 2 * a + b],
            recv_sem=direct_recv,
            device_id=device(y, hi, to_core, to_z, to_xl),
            device_id_type=MESH,
        )

    def direct(hi):
        products(last, hi)
        for k in far_first:
            for a in range(2):
                for b in range(2):
                    direct_copy(hi, k, a, b).start()
        for a, b in ((1, 0), (1, 1), (0, 1)):
            direct_copy(hi, 0, a, b).start()

        @pl.when(xh != hi)
        def _():
            direct_copy(hi, 0, 0, 0).start()

        @pl.when(xh == hi)
        def _():
            pltpu.make_async_copy(
                packed.at[2 * last + hi, z, core, xl], landed.at[last, own_source, z], direct_recv
            ).start()

    def wait_direct():
        pltpu.make_async_copy(landed.at[last], landed.at[last], direct_recv).wait()

    def wait_row(n):
        for k, (e, a, b) in enumerate(row):
            here = landed.at[n, 4 * ((xh + e) % 2) + 2 * ((xl + a) % 2) + (core + b) % 2]
            pltpu.make_async_copy(here, here, row_recv.at[n, k]).wait()

    span = 2 * rows_z * 16

    def sort(n):
        def one(group, carry):
            lo, depth = group // rows_z, group % rows_z
            tiles = [landed[n, 4 * (s // 2) + 2 * lo + s % 2, depth].astype(F32) for s in range(4)]
            at = pl.multiple_of(n * span + group * 16, 16)
            for h in range(2):
                for r in range(ROUNDS):
                    parts = []
                    for c in range(2):
                        value = None
                        for s in range(4):
                            turned = tiles[s][8 * c : 8 * c + 8]
                            amount = 2 * (s - (2 * h + r)) % 8
                            if amount:
                                turned = pltpu.roll(turned, amount, 0)
                            value = turned if value is None else jnp.where(sublane < 2 * s, value, turned)
                        parts.append(value)
                    sorted_[r, pl.ds(at, 16), h * LANES : (h + 1) * LANES] = jnp.concatenate(parts, 0).astype(BF16)
            return carry

        lax.fori_loop(0, 2 * rows_z, one, 0)

    def lag_product(first, stop):
        rows = pl.ds(first * span, (stop - first) * span)

        def one(r, carry):
            value = lax.dot_general(
                sorted_[r, rows, :], table[rows, :], (((0,), (0,)), ((), ())), preferred_element_type=F32
            )
            if stop < CHUNKS:
                total[r] = value
            else:
                out[r, 0] = (total[r] + value).astype(BF16)
            return carry

        lax.fori_loop(0, ROUNDS, one, 0)

    def wait_y(n):
        for p in range(len(pieces[n])):
            y_copy(n, p).wait_recv()

    for p in range(len(pieces[0])):
        forward(0, p)
    wave(0, 1)
    for n in range(last):
        half_way = len(pieces[n + 1]) // 2
        for p in range(half_way):
            forward(n + 1, p)
        wait_y(n)
        wave(n, 0)
        for p in range(half_way, len(pieces[n + 1])):
            forward(n + 1, p)
        if n + 1 < last:
            wave(n + 1, 1)
    direct(1)
    for n in range(last):
        for hi in (1, 0):
            send_row(n, hi)
    wait_y(last)
    direct(0)
    for n in range(last):
        wait_row(n)
        sort(n)
    lag_product(0, last)
    wait_direct()
    sort(last)
    lag_product(last, CHUNKS)

    for copy in x_copies:
        copy.wait_send()
    for n in range(CHUNKS):
        for p in range(len(pieces[n])):
            y_copy(n, p).wait_send()
    for hi in range(2):
        for n in range(last):
            for k in range(1, rows_z):
                z_copy(n, hi, k).wait_send()
            for a, b in ((1, 0), (1, 1), (0, 1)):
                row_copy(n, hi, a, b).wait_send()
        for k in range(rows_z):
            for a in range(2):
                for b in range(2):
                    if (k, a, b) != (0, 0, 0):
                        direct_copy(hi, k, a, b).wait_send()

        @pl.when(xh != hi)
        def _():
            direct_copy(hi, 0, 0, 0).wait_send()
            for n in range(last):
                row_copy(n, hi, 0, 0).wait_send()


def in_hbm(array):
    return pltpu.with_memory_space_constraint(array, pltpu.HBM)


def local(rows_y, rows_z, spectra, band_weight):
    _, freqs, windows, width = spectra.shape
    bins = band_weight.shape[0]
    lags = 2 * bins
    pairs = (width // 2) ** 2 // (2 * rows_z)
    held_freqs = CHUNKS * RUN
    rows = CHUNKS * 2 * rows_z * 16
    dma = pltpu.SemaphoreType.DMA
    return pl.pallas_call(
        functools.partial(stack_kernel, rows_y, rows_z),
        name="stack",
        out_shape=jax.ShapeDtypeStruct((ROUNDS, 1, pairs, lags), BF16),
        in_specs=[pl.BlockSpec(memory_space=pltpu.HBM), pl.BlockSpec(memory_space=pltpu.HBM)],
        out_specs=pl.BlockSpec(memory_space=pltpu.VMEM),
        scratch_shapes=[
            pltpu.VMEM((bins // LANES, LANES), F32),
            pltpu.VMEM((6, held_freqs, windows, width), BF16),
            pltpu.VMEM((rows, lags), BF16),
            pltpu.VMEM((bins, LANES), F32),
            pltpu.VMEM((2 * ROUNDS * RUN * width // 2, width), F32),
            pltpu.VMEM((2 * CHUNKS, rows_z, 2, 2, 16, LANES), BF16),
            pltpu.VMEM((2 * CHUNKS, rows_z, 2, 2, 16, LANES), BF16),
            pltpu.VMEM((CHUNKS, 8, rows_z, 16, LANES), BF16),
            pltpu.VMEM((ROUNDS, rows, pairs), BF16),
            pltpu.VMEM((ROUNDS, pairs, lags), F32),
            dma((CHUNKS, 2 * RUN, 4)),
            dma((CHUNKS, 2 * RUN, 4)),
            dma((CHUNKS, 2 * RUN)),
            dma((CHUNKS, 2 * RUN)),
            dma((2 * CHUNKS, rows_z)),
            dma((2 * CHUNKS, rows_z)),
            dma((CHUNKS, 2, 4)),
            dma((CHUNKS, 8)),
            dma((2, rows_z, 4)),
            dma,
            dma,
        ],
        compiler_params=pltpu.CompilerParams(
            collective_id=0, has_side_effects=True, vmem_limit_bytes=48 * 2**20
        ),
    )(in_hbm(spectra), in_hbm(band_weight.reshape(bins // LANES, LANES)))


def solution(mesh):
    rows_y, rows_z = mesh.shape["grp"] // 4, mesh.shape["frq"] // 2
    return jax.shard_map(
        functools.partial(local, rows_y, rows_z),
        mesh=mesh,
        in_specs=(P("grp", "frq", None, None), P()),
        out_specs=P(None, "grp", "frq", None),
        check_vma=False,
    )
```

```python
import functools
import math

import jax
import jax.numpy as jnp
from jax import lax
from jax.experimental import pallas as pl
from jax.experimental.pallas import tpu as pltpu
from jax.sharding import PartitionSpec as P

ROUNDS = 2
CHUNKS = 4
RUN = 2
LANES = 128
MESH = pl.DeviceIdType.MESH
F32 = jnp.float32
BF16 = jnp.bfloat16


def stack_kernel(
    rows_y, rows_z, spectra, weight_in, out, weight, held, table, weights, work, packed, relay, landed, sorted_, total,
    x_send, x_recv, y_send, y_recv, z_send, z_recv, row_send, row_recv, direct_send, direct_recv, own_sem, row_here, plane_here,
):
    grp, frq = lax.axis_index("grp"), lax.axis_index("frq")
    y, xh, core = grp // 4, (grp // 2) % 2, grp % 2
    z, xl = frq // 2, frq % 2

    def device(y_, xh_, core_, z_, xl_):
        return (y_ * 4 + xh_ * 2 + core_, z_ * 2 + xl_)

    up, down = (y + 1) % rows_y, (y + rows_y - 1) % rows_y
    row = [(e, a, b) for e in range(2) for a in range(2) for b in range(2)]

    def in_plane(k, e, a, b):
        return device(y, (xh + e) % 2, (core + b) % 2, (z + k) % rows_z, (xl + a) % 2)

    windows, width = held.shape[2], held.shape[3]
    whole, halves = [(0, windows)], [(0, LANES), (LANES, windows - LANES)]
    pieces = [
        [(n * RUN + f, *cut) for f in range(RUN) for cut in (halves if n == CHUNKS - 1 else whole)]
        for n in range(CHUNKS)
    ]

    barrier = pltpu.get_barrier_semaphore()
    own_source = 4 * xh + 2 * xl + core
    leads = own_source == 0

    def say(semaphore, who):
        pl.semaphore_signal(semaphore, inc=1, device_id=who, device_id_type=MESH)

    for e, a, b in row[1:]:
        @pl.when(4 * ((xh + e) % 2) + 2 * ((xl + a) % 2) + (core + b) % 2 != 0)
        def _():
            say(barrier, in_plane(0, e, a, b))
    say(barrier, device(up, xh, core, z, xl))
    say(barrier, device(down, xh, core, z, xl))

    @pl.when(jnp.logical_not(leads))
    def _():
        pl.semaphore_wait(barrier, 9)
        say(row_here, device(y, 0, 0, z, 0))

    @pl.when(leads)
    def _():
        pl.semaphore_wait(row_here, 7)

    weight_copy = pltpu.make_async_copy(weight_in, weight, own_sem)
    weight_copy.start()

    x_copies = []
    for n in range(CHUNKS):
        for p, (f, row_first, row_count) in enumerate(pieces[n]):
            for e in range(2):
                for b in range(2):
                    to_xh, to_core = (xh + e) % 2, (core + b) % 2
                    source = n * 3 * RUN + RUN * (2 * to_xh + to_core) + f
                    copy = pltpu.make_async_remote_copy(
                        src_ref=spectra.at[0, source, pl.ds(row_first, row_count)],
                        dst_ref=held.at[2 + 2 * xh + core, f, pl.ds(row_first, row_count)],
                        send_sem=x_send.at[n, p, 2 * e + b],
                        recv_sem=x_recv.at[n, p, 2 * e + b],
                        device_id=device(y, to_xh, to_core, z, 1 - xl),
                        device_id_type=MESH,
                    )
                    copy.start()
                    x_copies.append(copy)

    @pl.when(leads)
    def _():
        for k in range(1, rows_z):
            say(barrier, in_plane(k, 0, 0, 0))

    def wait_x(n, p):
        f, row_first, row_count = pieces[n][p]
        for e in range(2):
            for b in range(2):
                slot = 2 + 2 * ((xh + e) % 2) + (core + b) % 2
                here = held.at[slot, f, pl.ds(row_first, row_count)]
                pltpu.make_async_copy(here, here, x_recv.at[n, p, 2 * e + b]).wait()

    def y_copy(n, p):
        f, row_first, row_count = pieces[n][p]
        return pltpu.make_async_remote_copy(
            src_ref=held.at[pl.ds(4, 2), f, pl.ds(row_first, row_count)],
            dst_ref=held.at[pl.ds(0, 2), f, pl.ds(row_first, row_count)],
            send_sem=y_send.at[n, p],
            recv_sem=y_recv.at[n, p],
            device_id=device(up, xh, core, z, xl),
            device_id_type=MESH,
        )

    def forward(n, p):
        wait_x(n, p)
        y_copy(n, p).start()

    lags = table.shape[1]
    bins = lags // 2
    weight_copy.wait()
    for b in range(bins // LANES):
        wide = jnp.broadcast_to(weight[b : b + 1, :], (LANES, LANES))
        weights[pl.ds(b * LANES, LANES), :] = wide.T * (1.0 / math.sqrt(bins))

    group_rows = lax.broadcasted_iota(jnp.int32, (8, LANES), 0)
    group_cols = lax.broadcasted_iota(jnp.int32, (8, LANES), 1)
    turn = 2.0 * math.pi / lags
    steps = []
    for s in range(lags // LANES):
        angle = ((group_rows * (s * LANES)) % lags).astype(F32) * turn
        steps.append((jnp.cos(angle), jnp.sin(angle)))

    def table_rows(index, carry):
        n, group = index // (2 * rows_z), index % (2 * rows_z)
        lo, depth = group // rows_z, group % rows_z
        first = pl.multiple_of(depth * 64 + (1 - lo) * 32 + n * 8, 8)
        angle = (((group_rows + first) * group_cols) % lags).astype(F32) * turn
        scale = weights[pl.ds(first, 8), :]
        base_cos, base_sin = jnp.cos(angle) * scale, jnp.sin(angle) * scale
        at = pl.multiple_of(index * 16, 16)
        for s, (step_cos, step_sin) in enumerate(steps):
            real = base_cos * step_cos - base_sin * step_sin
            imag = base_sin * step_cos + base_cos * step_sin
            table[pl.ds(at, 16), s * LANES : (s + 1) * LANES] = jnp.concatenate([real, -imag], 0).astype(BF16)
        return carry

    lax.fori_loop(0, CHUNKS * 2 * rows_z, table_rows, 0)

    @pl.when(leads)
    def _():
        pl.semaphore_wait(barrier, 2 + rows_z - 1)
        for e, a, b in row[1:]:
            say(plane_here, in_plane(0, e, a, b))

    half = width // 2
    lane = lax.broadcasted_iota(jnp.int32, (8, LANES), 1) < half
    sublane = lax.broadcasted_iota(jnp.int32, (8, LANES), 0)
    sign = jnp.where(lax.broadcasted_iota(jnp.int32, (half, width), 1) < half, 1.0, -1.0)

    def products(n, hi):
        for c_to in range(2):
            m = 2 * hi + c_to
            for f in range(RUN):
                at = n * RUN + f
                pair = jnp.concatenate([held[m + 1, at], held[m, at]], 1)
                product = lax.dot_general(
                    held[m + 2, at], pair, (((0,), (0,)), ((), ())), preferred_element_type=F32
                ) * (1.0 / math.sqrt(windows))
                for r in range(ROUNDS):
                    block = product[:, r * width : (r + 1) * width]
                    both = block[:half] * sign + pltpu.roll(block[half:], half, 1)
                    work[pl.ds(((c_to * ROUNDS + r) * RUN + f) * half, half), :] = both
        for shard in range(half // 4):
            real, imag = [], []
            for h in range(2):
                first = work[pl.ds(4 * shard + 2 * h, 8, stride=half), :]
                second = work[pl.ds(4 * shard + 2 * h + 1, 8, stride=half), :]
                real.append(jnp.where(lane, first, pltpu.roll(second, half, 1)))
                imag.append(jnp.where(lane, pltpu.roll(first, half, 1), second))
            for c_to in range(2):
                parts = []
                for lower, upper in (real, imag):
                    if c_to:
                        lower = pltpu.roll(lower, 4, 0)
                    else:
                        upper = pltpu.roll(upper, 4, 0)
                    parts.append(jnp.where(sublane < 4, lower, upper))
                packed[2 * n + hi, shard // 2, c_to, shard % 2] = jnp.concatenate(parts, 0).astype(BF16)

    last = CHUNKS - 1
    far_first = sorted(range(1, rows_z), key=lambda k: -min(k, rows_z - k))

    def z_copy(n, hi, k):
        w = 2 * n + hi
        return pltpu.make_async_remote_copy(
            src_ref=packed.at[w, (z + k) % rows_z],
            dst_ref=relay.at[w, z],
            send_sem=z_send.at[w, k],
            recv_sem=z_recv.at[w, k],
            device_id=device(y, xh, core, (z + k) % rows_z, xl),
            device_id_type=MESH,
        )

    def send_z(n, hi):
        for k in far_first:
            z_copy(n, hi, k).start()
        w = 2 * n + hi
        pltpu.make_async_copy(packed.at[w, z], relay.at[w, z], z_recv.at[w, 0]).start()

    def wave(n, hi):
        products(n, hi)
        send_z(n, hi)

    def wait_z(n, hi):
        w = 2 * n + hi
        for k in range(rows_z):
            here = relay.at[w, (z + rows_z - k) % rows_z]
            pltpu.make_async_copy(here, here, z_recv.at[w, k]).wait()

    def row_copy(n, hi, a, b):
        return pltpu.make_async_remote_copy(
            src_ref=relay.at[2 * n + hi, :, (core + b) % 2, (xl + a) % 2],
            dst_ref=landed.at[n, own_source],
            send_sem=row_send.at[n, hi, 2 * a + b],
            recv_sem=row_recv.at[n, 4 * ((xh + hi) % 2) + 2 * a + b],
            device_id=device(y, hi, (core + b) % 2, z, (xl + a) % 2),
            device_id_type=MESH,
        )

    def send_row(n, hi):
        wait_z(n, hi)
        for a, b in ((1, 0), (1, 1), (0, 1)):
            row_copy(n, hi, a, b).start()

        @pl.when(xh != hi)
        def _():
            row_copy(n, hi, 0, 0).start()

        @pl.when(xh == hi)
        def _():
            pltpu.make_async_copy(
                relay.at[2 * n + hi, :, core, xl], landed.at[n, own_source], row_recv.at[n, 0]
            ).start()

    def direct_copy(hi, k, a, b):
        to_z, to_core, to_xl = (z + k) % rows_z, (core + b) % 2, (xl + a) % 2
        return pltpu.make_async_remote_copy(
            src_ref=packed.at[2 * last + hi, to_z, to_core, to_xl],
            dst_ref=landed.at[last, own_source, z],
            send_sem=direct_send.at[hi, k, 2 * a + b],
            recv_sem=direct_recv,
            device_id=device(y, hi, to_core, to_z, to_xl),
            device_id_type=MESH,
        )

    def direct(hi):
        products(last, hi)
        for k in far_first:
            for a in range(2):
                for b in range(2):
                    direct_copy(hi, k, a, b).start()
        for a, b in ((1, 0), (1, 1), (0, 1)):
            direct_copy(hi, 0, a, b).start()

        @pl.when(xh != hi)
        def _():
            direct_copy(hi, 0, 0, 0).start()

        @pl.when(xh == hi)
        def _():
            pltpu.make_async_copy(
                packed.at[2 * last + hi, z, core, xl], landed.at[last, own_source, z], direct_recv
            ).start()

    def wait_direct():
        pltpu.make_async_copy(landed.at[last], landed.at[last], direct_recv).wait()

    def wait_row(n):
        for k, (e, a, b) in enumerate(row):
            here = landed.at[n, 4 * ((xh + e) % 2) + 2 * ((xl + a) % 2) + (core + b) % 2]
            pltpu.make_async_copy(here, here, row_recv.at[n, k]).wait()

    span = 2 * rows_z * 16

    def sort(n):
        def one(group, carry):
            lo, depth = group // rows_z, group % rows_z
            tiles = [landed[n, 4 * (s // 2) + 2 * lo + s % 2, depth].astype(F32) for s in range(4)]
            at = pl.multiple_of(n * span + group * 16, 16)
            for h in range(2):
                for r in range(ROUNDS):
                    parts = []
                    for c in range(2):
                        value = None
                        for s in range(4):
                            turned = tiles[s][8 * c : 8 * c + 8]
                            amount = 2 * (s - (2 * h + r)) % 8
                            if amount:
                                turned = pltpu.roll(turned, amount, 0)
                            value = turned if value is None else jnp.where(sublane < 2 * s, value, turned)
                        parts.append(value)
                    sorted_[r, pl.ds(at, 16), h * LANES : (h + 1) * LANES] = jnp.concatenate(parts, 0).astype(BF16)
            return carry

        lax.fori_loop(0, 2 * rows_z, one, 0)

    def lag_product(first, stop):
        rows = pl.ds(first * span, (stop - first) * span)

        def one(r, carry):
            value = lax.dot_general(
                sorted_[r, rows, :], table[rows, :], (((0,), (0,)), ((), ())), preferred_element_type=F32
            )
            if stop < CHUNKS:
                total[r] = value
            else:
                out[r, 0] = (total[r] + value).astype(BF16)
            return carry

        lax.fori_loop(0, ROUNDS, one, 0)

    def wait_y(n):
        for p in range(len(pieces[n])):
            y_copy(n, p).wait_recv()

    for p in range(len(pieces[0])):
        forward(0, p)
    products(0, 1)

    @pl.when(jnp.logical_not(leads))
    def _():
        pl.semaphore_wait(plane_here, 1)

    send_z(0, 1)
    for n in range(last):
        half_way = len(pieces[n + 1]) // 2
        for p in range(half_way):
            forward(n + 1, p)
        wait_y(n)
        wave(n, 0)
        if n + 1 == last:
            pass
            send_row(0, 1)
            send_row(0, 0)
            send_row(1, 1)
            send_row(1, 0)
        for p in range(half_way, len(pieces[n + 1])):
            forward(n + 1, p)
        if n + 1 < last:
            wave(n + 1, 1)
    direct(1)
    send_row(2, 1)
    send_row(2, 0)
    wait_y(last)
    direct(0)
    for n in range(last):
        wait_row(n)
        sort(n)
    lag_product(0, last)
    wait_direct()
    sort(last)
    lag_product(last, CHUNKS)

    for copy in x_copies:
        copy.wait_send()
    for n in range(CHUNKS):
        for p in range(len(pieces[n])):
            y_copy(n, p).wait_send()
    for hi in range(2):
        for n in range(last):
            for k in range(1, rows_z):
                z_copy(n, hi, k).wait_send()
            for a, b in ((1, 0), (1, 1), (0, 1)):
                row_copy(n, hi, a, b).wait_send()
        for k in range(rows_z):
            for a in range(2):
                for b in range(2):
                    if (k, a, b) != (0, 0, 0):
                        direct_copy(hi, k, a, b).wait_send()

        @pl.when(xh != hi)
        def _():
            direct_copy(hi, 0, 0, 0).wait_send()
            for n in range(last):
                row_copy(n, hi, 0, 0).wait_send()


def in_hbm(array):
    return pltpu.with_memory_space_constraint(array, pltpu.HBM)


def local(rows_y, rows_z, spectra, band_weight):
    _, freqs, windows, width = spectra.shape
    bins = band_weight.shape[0]
    lags = 2 * bins
    pairs = (width // 2) ** 2 // (2 * rows_z)
    held_freqs = CHUNKS * RUN
    rows = CHUNKS * 2 * rows_z * 16
    dma = pltpu.SemaphoreType.DMA
    return pl.pallas_call(
        functools.partial(stack_kernel, rows_y, rows_z),
        name="stack",
        out_shape=jax.ShapeDtypeStruct((ROUNDS, 1, pairs, lags), BF16),
        in_specs=[pl.BlockSpec(memory_space=pltpu.HBM), pl.BlockSpec(memory_space=pltpu.HBM)],
        out_specs=pl.BlockSpec(memory_space=pltpu.VMEM),
        scratch_shapes=[
            pltpu.VMEM((bins // LANES, LANES), F32),
            pltpu.VMEM((6, held_freqs, windows, width), BF16),
            pltpu.VMEM((rows, lags), BF16),
            pltpu.VMEM((bins, LANES), F32),
            pltpu.VMEM((2 * ROUNDS * RUN * width // 2, width), F32),
            pltpu.VMEM((2 * CHUNKS, rows_z, 2, 2, 16, LANES), BF16),
            pltpu.VMEM((2 * CHUNKS, rows_z, 2, 2, 16, LANES), BF16),
            pltpu.VMEM((CHUNKS, 8, rows_z, 16, LANES), BF16),
            pltpu.VMEM((ROUNDS, rows, pairs), BF16),
            pltpu.VMEM((ROUNDS, pairs, lags), F32),
            dma((CHUNKS, 2 * RUN, 4)),
            dma((CHUNKS, 2 * RUN, 4)),
            dma((CHUNKS, 2 * RUN)),
            dma((CHUNKS, 2 * RUN)),
            dma((2 * CHUNKS, rows_z)),
            dma((2 * CHUNKS, rows_z)),
            dma((CHUNKS, 2, 4)),
            dma((CHUNKS, 8)),
            dma((2, rows_z, 4)),
            dma,
            dma,
            pltpu.SemaphoreType.REGULAR,
            pltpu.SemaphoreType.REGULAR,
        ],
        compiler_params=pltpu.CompilerParams(
            collective_id=0, has_side_effects=True, vmem_limit_bytes=48 * 2**20
        ),
    )(in_hbm(spectra), in_hbm(band_weight.reshape(bins // LANES, LANES)))


def solution(mesh):
    rows_y, rows_z = mesh.shape["grp"] // 4, mesh.shape["frq"] // 2
    return jax.shard_map(
        functools.partial(local, rows_y, rows_z),
        mesh=mesh,
        in_specs=(P("grp", "frq", None, None), P()),
        out_specs=P(None, "grp", "frq", None),
        check_vma=False,
    )
```

```python
import functools
import math

import jax
import jax.numpy as jnp
from jax import lax
from jax.experimental import pallas as pl
from jax.experimental.pallas import tpu as pltpu
from jax.sharding import PartitionSpec as P

ROUNDS = 2
CHUNKS = 4
RUN = 2
DIRECT = 2
LANES = 128
MESH = pl.DeviceIdType.MESH
F32 = jnp.float32
BF16 = jnp.bfloat16


def stack_kernel(
    rows_y, rows_z, spectra, weight_in, out, weight, held, table, weights, work, packed, relay, landed, sorted_, total,
    x_send, x_recv, y_send, y_recv, z_send, z_recv, row_send, row_recv, direct_send, direct_recv, own_sem, row_here, plane_here,
):
    grp, frq = lax.axis_index("grp"), lax.axis_index("frq")
    y, xh, core = grp // 4, (grp // 2) % 2, grp % 2
    z, xl = frq // 2, frq % 2

    def device(y_, xh_, core_, z_, xl_):
        return (y_ * 4 + xh_ * 2 + core_, z_ * 2 + xl_)

    up, down = (y + 1) % rows_y, (y + rows_y - 1) % rows_y
    row = [(e, a, b) for e in range(2) for a in range(2) for b in range(2)]

    def in_plane(k, e, a, b):
        return device(y, (xh + e) % 2, (core + b) % 2, (z + k) % rows_z, (xl + a) % 2)

    windows, width = held.shape[2], held.shape[3]
    whole, halves = [(0, windows)], [(0, LANES), (LANES, windows - LANES)]
    pieces = [
        [(n * RUN + f, *cut) for f in range(RUN) for cut in (halves if n == CHUNKS - 1 else whole)]
        for n in range(CHUNKS)
    ]

    barrier = pltpu.get_barrier_semaphore()
    own_source = 4 * xh + 2 * xl + core
    leads = own_source == 0

    def say(semaphore, who):
        pl.semaphore_signal(semaphore, inc=1, device_id=who, device_id_type=MESH)

    for e, a, b in row[1:]:
        @pl.when(4 * ((xh + e) % 2) + 2 * ((xl + a) % 2) + (core + b) % 2 != 0)
        def _():
            say(barrier, in_plane(0, e, a, b))
    say(barrier, device(up, xh, core, z, xl))
    say(barrier, device(down, xh, core, z, xl))

    @pl.when(jnp.logical_not(leads))
    def _():
        pl.semaphore_wait(barrier, 9)
        say(row_here, device(y, 0, 0, z, 0))

    @pl.when(leads)
    def _():
        pl.semaphore_wait(row_here, 7)

    weight_copy = pltpu.make_async_copy(weight_in, weight, own_sem)
    weight_copy.start()

    x_copies = []
    for n in range(CHUNKS):
        for p, (f, row_first, row_count) in enumerate(pieces[n]):
            for e in range(2):
                for b in range(2):
                    to_xh, to_core = (xh + e) % 2, (core + b) % 2
                    source = n * 3 * RUN + RUN * (2 * to_xh + to_core) + f
                    copy = pltpu.make_async_remote_copy(
                        src_ref=spectra.at[0, source, pl.ds(row_first, row_count)],
                        dst_ref=held.at[2 + 2 * xh + core, f, pl.ds(row_first, row_count)],
                        send_sem=x_send.at[n, p, 2 * e + b],
                        recv_sem=x_recv.at[n, p, 2 * e + b],
                        device_id=device(y, to_xh, to_core, z, 1 - xl),
                        device_id_type=MESH,
                    )
                    copy.start()
                    x_copies.append(copy)

    @pl.when(leads)
    def _():
        for k in range(1, rows_z):
            say(barrier, in_plane(k, 0, 0, 0))

    def wait_x(n, p):
        f, row_first, row_count = pieces[n][p]
        for e in range(2):
            for b in range(2):
                slot = 2 + 2 * ((xh + e) % 2) + (core + b) % 2
                here = held.at[slot, f, pl.ds(row_first, row_count)]
                pltpu.make_async_copy(here, here, x_recv.at[n, p, 2 * e + b]).wait()

    def y_copy(n, p):
        f, row_first, row_count = pieces[n][p]
        return pltpu.make_async_remote_copy(
            src_ref=held.at[pl.ds(4, 2), f, pl.ds(row_first, row_count)],
            dst_ref=held.at[pl.ds(0, 2), f, pl.ds(row_first, row_count)],
            send_sem=y_send.at[n, p],
            recv_sem=y_recv.at[n, p],
            device_id=device(up, xh, core, z, xl),
            device_id_type=MESH,
        )

    def forward(n, p):
        wait_x(n, p)
        y_copy(n, p).start()

    lags = table.shape[1]
    bins = lags // 2
    weight_copy.wait()
    for b in range(bins // LANES):
        wide = jnp.broadcast_to(weight[b : b + 1, :], (LANES, LANES))
        weights[pl.ds(b * LANES, LANES), :] = wide.T * (1.0 / math.sqrt(bins))

    group_rows = lax.broadcasted_iota(jnp.int32, (8, LANES), 0)
    group_cols = lax.broadcasted_iota(jnp.int32, (8, LANES), 1)
    turn = 2.0 * math.pi / lags
    steps = []
    for s in range(lags // LANES):
        angle = ((group_rows * (s * LANES)) % lags).astype(F32) * turn
        steps.append((jnp.cos(angle), jnp.sin(angle)))

    def table_rows(index, carry):
        n, group = index // (2 * rows_z), index % (2 * rows_z)
        lo, depth = group // rows_z, group % rows_z
        first = pl.multiple_of(depth * 64 + (1 - lo) * 32 + n * 8, 8)
        angle = (((group_rows + first) * group_cols) % lags).astype(F32) * turn
        scale = weights[pl.ds(first, 8), :]
        base_cos, base_sin = jnp.cos(angle) * scale, jnp.sin(angle) * scale
        at = pl.multiple_of(index * 16, 16)
        for s, (step_cos, step_sin) in enumerate(steps):
            real = base_cos * step_cos - base_sin * step_sin
            imag = base_sin * step_cos + base_cos * step_sin
            table[pl.ds(at, 16), s * LANES : (s + 1) * LANES] = jnp.concatenate([real, -imag], 0).astype(BF16)
        return carry

    lax.fori_loop(0, CHUNKS * 2 * rows_z, table_rows, 0)

    @pl.when(leads)
    def _():
        pl.semaphore_wait(barrier, 2 + rows_z - 1)
        for e, a, b in row[1:]:
            say(plane_here, in_plane(0, e, a, b))

    half = width // 2
    lane = lax.broadcasted_iota(jnp.int32, (8, LANES), 1) < half
    sublane = lax.broadcasted_iota(jnp.int32, (8, LANES), 0)
    sign = jnp.where(lax.broadcasted_iota(jnp.int32, (half, width), 1) < half, 1.0, -1.0)

    def products(n, hi):
        for c_to in range(2):
            m = 2 * hi + c_to
            for f in range(RUN):
                at = n * RUN + f
                pair = jnp.concatenate([held[m + 1, at], held[m, at]], 1)
                product = lax.dot_general(
                    held[m + 2, at], pair, (((0,), (0,)), ((), ())), preferred_element_type=F32
                ) * (1.0 / math.sqrt(windows))
                for r in range(ROUNDS):
                    block = product[:, r * width : (r + 1) * width]
                    both = block[:half] * sign + pltpu.roll(block[half:], half, 1)
                    work[pl.ds(((c_to * ROUNDS + r) * RUN + f) * half, half), :] = both
        for shard in range(half // 4):
            real, imag = [], []
            for h in range(2):
                first = work[pl.ds(4 * shard + 2 * h, 8, stride=half), :]
                second = work[pl.ds(4 * shard + 2 * h + 1, 8, stride=half), :]
                real.append(jnp.where(lane, first, pltpu.roll(second, half, 1)))
                imag.append(jnp.where(lane, pltpu.roll(first, half, 1), second))
            for c_to in range(2):
                parts = []
                for lower, upper in (real, imag):
                    if c_to:
                        lower = pltpu.roll(lower, 4, 0)
                    else:
                        upper = pltpu.roll(upper, 4, 0)
                    parts.append(jnp.where(sublane < 4, lower, upper))
                packed[2 * n + hi, shard // 2, c_to, shard % 2] = jnp.concatenate(parts, 0).astype(BF16)

    last = CHUNKS - 1
    relayed = CHUNKS - DIRECT
    far_first = sorted(range(1, rows_z), key=lambda k: -min(k, rows_z - k))

    def z_copy(n, hi, k):
        w = 2 * n + hi
        return pltpu.make_async_remote_copy(
            src_ref=packed.at[w, (z + k) % rows_z],
            dst_ref=relay.at[w, z],
            send_sem=z_send.at[w, k],
            recv_sem=z_recv.at[w, k],
            device_id=device(y, xh, core, (z + k) % rows_z, xl),
            device_id_type=MESH,
        )

    def send_z(n, hi):
        for k in far_first:
            z_copy(n, hi, k).start()
        w = 2 * n + hi
        pltpu.make_async_copy(packed.at[w, z], relay.at[w, z], z_recv.at[w, 0]).start()

    def wait_z(n, hi):
        w = 2 * n + hi
        for k in range(rows_z):
            here = relay.at[w, (z + rows_z - k) % rows_z]
            pltpu.make_async_copy(here, here, z_recv.at[w, k]).wait()

    def row_copy(n, hi, a, b):
        return pltpu.make_async_remote_copy(
            src_ref=relay.at[2 * n + hi, :, (core + b) % 2, (xl + a) % 2],
            dst_ref=landed.at[n, own_source],
            send_sem=row_send.at[n, hi, 2 * a + b],
            recv_sem=row_recv.at[n, 4 * ((xh + hi) % 2) + 2 * a + b],
            device_id=device(y, hi, (core + b) % 2, z, (xl + a) % 2),
            device_id_type=MESH,
        )

    def send_row(n, hi):
        wait_z(n, hi)
        for a, b in ((1, 0), (1, 1), (0, 1)):
            row_copy(n, hi, a, b).start()

        @pl.when(xh != hi)
        def _():
            row_copy(n, hi, 0, 0).start()

        @pl.when(xh == hi)
        def _():
            pltpu.make_async_copy(
                relay.at[2 * n + hi, :, core, xl], landed.at[n, own_source], row_recv.at[n, 0]
            ).start()

    def direct_copy(n, hi, k, a, b):
        to_z, to_core, to_xl = (z + k) % rows_z, (core + b) % 2, (xl + a) % 2
        return pltpu.make_async_remote_copy(
            src_ref=packed.at[2 * n + hi, to_z, to_core, to_xl],
            dst_ref=landed.at[n, own_source, z],
            send_sem=direct_send.at[n - relayed, hi, k, 2 * a + b],
            recv_sem=direct_recv.at[n - relayed],
            device_id=device(y, hi, to_core, to_z, to_xl),
            device_id_type=MESH,
        )

    def send_direct(n, hi):
        for k in far_first:
            for a in range(2):
                for b in range(2):
                    direct_copy(n, hi, k, a, b).start()
        for a, b in ((1, 0), (1, 1), (0, 1)):
            direct_copy(n, hi, 0, a, b).start()

        @pl.when(xh != hi)
        def _():
            direct_copy(n, hi, 0, 0, 0).start()

        @pl.when(xh == hi)
        def _():
            pltpu.make_async_copy(
                packed.at[2 * n + hi, z, core, xl], landed.at[n, own_source, z], direct_recv.at[n - relayed]
            ).start()

    def wait_direct(n):
        pltpu.make_async_copy(landed.at[n], landed.at[n], direct_recv.at[n - relayed]).wait()

    def send_wave(n, hi):
        if n < relayed:
            send_z(n, hi)
        else:
            send_direct(n, hi)

    def wave(n, hi):
        products(n, hi)
        send_wave(n, hi)

    def wait_row(n):
        for k, (e, a, b) in enumerate(row):
            here = landed.at[n, 4 * ((xh + e) % 2) + 2 * ((xl + a) % 2) + (core + b) % 2]
            pltpu.make_async_copy(here, here, row_recv.at[n, k]).wait()

    span = 2 * rows_z * 16

    def sort(n):
        def one(group, carry):
            lo, depth = group // rows_z, group % rows_z
            tiles = [landed[n, 4 * (s // 2) + 2 * lo + s % 2, depth].astype(F32) for s in range(4)]
            at = pl.multiple_of(n * span + group * 16, 16)
            for h in range(2):
                for r in range(ROUNDS):
                    parts = []
                    for c in range(2):
                        value = None
                        for s in range(4):
                            turned = tiles[s][8 * c : 8 * c + 8]
                            amount = 2 * (s - (2 * h + r)) % 8
                            if amount:
                                turned = pltpu.roll(turned, amount, 0)
                            value = turned if value is None else jnp.where(sublane < 2 * s, value, turned)
                        parts.append(value)
                    sorted_[r, pl.ds(at, 16), h * LANES : (h + 1) * LANES] = jnp.concatenate(parts, 0).astype(BF16)
            return carry

        lax.fori_loop(0, 2 * rows_z, one, 0)

    def lag_product(first, stop):
        rows = pl.ds(first * span, (stop - first) * span)

        def one(r, carry):
            value = lax.dot_general(
                sorted_[r, rows, :], table[rows, :], (((0,), (0,)), ((), ())), preferred_element_type=F32
            )
            if stop < CHUNKS:
                total[r] = value
            else:
                out[r, 0] = (total[r] + value).astype(BF16)
            return carry

        lax.fori_loop(0, ROUNDS, one, 0)

    def wait_y(n):
        for p in range(len(pieces[n])):
            y_copy(n, p).wait_recv()

    for p in range(len(pieces[0])):
        forward(0, p)
    products(0, 1)

    @pl.when(jnp.logical_not(leads))
    def _():
        pl.semaphore_wait(plane_here, 1)

    send_wave(0, 1)
    for n in range(last):
        half_way = len(pieces[n + 1]) // 2
        for p in range(half_way):
            forward(n + 1, p)
        wait_y(n)
        wave(n, 0)
        if n + 1 == last:
            for early in range(min(2, relayed)):
                for hi in (1, 0):
                    send_row(early, hi)
        for p in range(half_way, len(pieces[n + 1])):
            forward(n + 1, p)
        wave(n + 1, 1)
    for early in range(2, relayed):
        for hi in (1, 0):
            send_row(early, hi)
    wait_y(last)
    wave(last, 0)
    for n in range(last):
        if n < relayed:
            wait_row(n)
        else:
            wait_direct(n)
        sort(n)
    lag_product(0, last)
    wait_direct(last)
    sort(last)
    lag_product(last, CHUNKS)

    for copy in x_copies:
        copy.wait_send()
    for n in range(CHUNKS):
        for p in range(len(pieces[n])):
            y_copy(n, p).wait_send()
    for n in range(CHUNKS):
        for hi in range(2):
            if n < relayed:
                for k in range(1, rows_z):
                    z_copy(n, hi, k).wait_send()
                for a, b in ((1, 0), (1, 1), (0, 1)):
                    row_copy(n, hi, a, b).wait_send()
            else:
                for k in range(rows_z):
                    for a in range(2):
                        for b in range(2):
                            if (k, a, b) != (0, 0, 0):
                                direct_copy(n, hi, k, a, b).wait_send()

            @pl.when(xh != hi)
            def _():
                if n < relayed:
                    row_copy(n, hi, 0, 0).wait_send()
                else:
                    direct_copy(n, hi, 0, 0, 0).wait_send()


def in_hbm(array):
    return pltpu.with_memory_space_constraint(array, pltpu.HBM)


def local(rows_y, rows_z, spectra, band_weight):
    _, freqs, windows, width = spectra.shape
    bins = band_weight.shape[0]
    lags = 2 * bins
    pairs = (width // 2) ** 2 // (2 * rows_z)
    held_freqs = CHUNKS * RUN
    rows = CHUNKS * 2 * rows_z * 16
    dma = pltpu.SemaphoreType.DMA
    return pl.pallas_call(
        functools.partial(stack_kernel, rows_y, rows_z),
        name="stack",
        out_shape=jax.ShapeDtypeStruct((ROUNDS, 1, pairs, lags), BF16),
        in_specs=[pl.BlockSpec(memory_space=pltpu.HBM), pl.BlockSpec(memory_space=pltpu.HBM)],
        out_specs=pl.BlockSpec(memory_space=pltpu.VMEM),
        scratch_shapes=[
            pltpu.VMEM((bins // LANES, LANES), F32),
            pltpu.VMEM((6, held_freqs, windows, width), BF16),
            pltpu.VMEM((rows, lags), BF16),
            pltpu.VMEM((bins, LANES), F32),
            pltpu.VMEM((2 * ROUNDS * RUN * width // 2, width), F32),
            pltpu.VMEM((2 * CHUNKS, rows_z, 2, 2, 16, LANES), BF16),
            pltpu.VMEM((2 * CHUNKS, rows_z, 2, 2, 16, LANES), BF16),
            pltpu.VMEM((CHUNKS, 8, rows_z, 16, LANES), BF16),
            pltpu.VMEM((ROUNDS, rows, pairs), BF16),
            pltpu.VMEM((ROUNDS, pairs, lags), F32),
            dma((CHUNKS, 2 * RUN, 4)),
            dma((CHUNKS, 2 * RUN, 4)),
            dma((CHUNKS, 2 * RUN)),
            dma((CHUNKS, 2 * RUN)),
            dma((2 * CHUNKS, rows_z)),
            dma((2 * CHUNKS, rows_z)),
            dma((CHUNKS, 2, 4)),
            dma((CHUNKS, 8)),
            dma((DIRECT, 2, rows_z, 4)),
            dma((DIRECT,)),
            dma,
            pltpu.SemaphoreType.REGULAR,
            pltpu.SemaphoreType.REGULAR,
        ],
        compiler_params=pltpu.CompilerParams(
            collective_id=0, has_side_effects=True, vmem_limit_bytes=48 * 2**20
        ),
    )(in_hbm(spectra), in_hbm(band_weight.reshape(bins // LANES, LANES)))


def solution(mesh):
    rows_y, rows_z = mesh.shape["grp"] // 4, mesh.shape["frq"] // 2
    return jax.shard_map(
        functools.partial(local, rows_y, rows_z),
        mesh=mesh,
        in_specs=(P("grp", "frq", None, None), P()),
        out_specs=P(None, "grp", "frq", None),
        check_vma=False,
    )
```

```python
import functools
import math

import jax
import jax.numpy as jnp
from jax import lax
from jax.experimental import pallas as pl
from jax.experimental.pallas import tpu as pltpu
from jax.sharding import PartitionSpec as P

ROUNDS = 2
CHUNKS = 4
RUN = 2
DIRECT = 2
LANES = 128
MESH = pl.DeviceIdType.MESH
F32 = jnp.float32
BF16 = jnp.bfloat16


def stack_kernel(
    rows_y, rows_z, spectra, weight_in, out, weight, held, table, weights, work, packed, relay, landed, sorted_, total,
    x_send, x_recv, y_send, y_recv, z_send, z_recv, row_send, row_recv, direct_send, direct_recv, own_sem, row_here, plane_here,
):
    grp, frq = lax.axis_index("grp"), lax.axis_index("frq")
    y, xh, core = grp // 4, (grp // 2) % 2, grp % 2
    z, xl = frq // 2, frq % 2

    def device(y_, xh_, core_, z_, xl_):
        return (y_ * 4 + xh_ * 2 + core_, z_ * 2 + xl_)

    up, down = (y + 1) % rows_y, (y + rows_y - 1) % rows_y
    row = [(e, a, b) for e in range(2) for a in range(2) for b in range(2)]

    def in_plane(k, e, a, b):
        return device(y, (xh + e) % 2, (core + b) % 2, (z + k) % rows_z, (xl + a) % 2)

    windows, width = held.shape[2], held.shape[3]
    whole, halves = [(0, windows)], [(0, LANES), (LANES, windows - LANES)]
    pieces = [
        [(n * RUN + f, *cut) for f in range(RUN) for cut in (halves if n == CHUNKS - 1 else whole)]
        for n in range(CHUNKS)
    ]

    barrier = pltpu.get_barrier_semaphore()
    own_source = 4 * xh + 2 * xl + core
    leads = own_source == 0

    def say(semaphore, who):
        pl.semaphore_signal(semaphore, inc=1, device_id=who, device_id_type=MESH)

    for e, a, b in row[1:]:
        @pl.when(4 * ((xh + e) % 2) + 2 * ((xl + a) % 2) + (core + b) % 2 != 0)
        def _():
            say(barrier, in_plane(0, e, a, b))
    say(barrier, device(up, xh, core, z, xl))
    say(barrier, device(down, xh, core, z, xl))

    @pl.when(jnp.logical_not(leads))
    def _():
        pl.semaphore_wait(barrier, 9)
        say(row_here, device(y, 0, 0, z, 0))

    @pl.when(leads)
    def _():
        pl.semaphore_wait(row_here, 7)

    weight_copy = pltpu.make_async_copy(weight_in, weight, own_sem)
    weight_copy.start()

    x_copies = []
    for n in range(CHUNKS):
        for p, (f, row_first, row_count) in enumerate(pieces[n]):
            for e in range(2):
                for b in range(2):
                    to_xh, to_core = (xh + e) % 2, (core + b) % 2
                    source = n * 3 * RUN + RUN * (2 * to_xh + to_core) + f
                    copy = pltpu.make_async_remote_copy(
                        src_ref=spectra.at[0, source, pl.ds(row_first, row_count)],
                        dst_ref=held.at[2 + 2 * xh + core, f, pl.ds(row_first, row_count)],
                        send_sem=x_send.at[n, p, 2 * e + b],
                        recv_sem=x_recv.at[n, p, 2 * e + b],
                        device_id=device(y, to_xh, to_core, z, 1 - xl),
                        device_id_type=MESH,
                    )
                    copy.start()
                    x_copies.append(copy)

    @pl.when(leads)
    def _():
        for k in range(1, rows_z):
            say(barrier, in_plane(k, 0, 0, 0))

    def wait_x(n, p):
        f, row_first, row_count = pieces[n][p]
        for e in range(2):
            for b in range(2):
                slot = 2 + 2 * ((xh + e) % 2) + (core + b) % 2
                here = held.at[slot, f, pl.ds(row_first, row_count)]
                pltpu.make_async_copy(here, here, x_recv.at[n, p, 2 * e + b]).wait()

    def y_copy(n, p):
        f, row_first, row_count = pieces[n][p]
        return pltpu.make_async_remote_copy(
            src_ref=held.at[pl.ds(4, 2), f, pl.ds(row_first, row_count)],
            dst_ref=held.at[pl.ds(0, 2), f, pl.ds(row_first, row_count)],
            send_sem=y_send.at[n, p],
            recv_sem=y_recv.at[n, p],
            device_id=device(up, xh, core, z, xl),
            device_id_type=MESH,
        )

    def forward(n, p):
        wait_x(n, p)
        y_copy(n, p).start()

    lags = table.shape[1]
    bins = lags // 2
    weight_copy.wait()
    for b in range(bins // LANES):
        wide = jnp.broadcast_to(weight[b : b + 1, :], (LANES, LANES))
        weights[pl.ds(b * LANES, LANES), :] = wide.T * (1.0 / math.sqrt(bins))

    group_rows = lax.broadcasted_iota(jnp.int32, (8, LANES), 0)
    group_cols = lax.broadcasted_iota(jnp.int32, (8, LANES), 1)
    turn = 2.0 * math.pi / lags
    steps = []
    for s in range(lags // LANES):
        angle = ((group_rows * (s * LANES)) % lags).astype(F32) * turn
        steps.append((jnp.cos(angle), jnp.sin(angle)))

    def table_rows(index, carry):
        n, group = index // (2 * rows_z), index % (2 * rows_z)
        lo, depth = group // rows_z, group % rows_z
        first = pl.multiple_of(depth * 64 + (1 - lo) * 32 + n * 8, 8)
        angle = (((group_rows + first) * group_cols) % lags).astype(F32) * turn
        scale = weights[pl.ds(first, 8), :]
        base_cos, base_sin = jnp.cos(angle) * scale, jnp.sin(angle) * scale
        at = pl.multiple_of(index * 16, 16)
        for s, (step_cos, step_sin) in enumerate(steps):
            real = base_cos * step_cos - base_sin * step_sin
            imag = base_sin * step_cos + base_cos * step_sin
            table[pl.ds(at, 16), s * LANES : (s + 1) * LANES] = jnp.concatenate([real, -imag], 0).astype(BF16)
        return carry

    lax.fori_loop(0, CHUNKS * 2 * rows_z, table_rows, 0)

    @pl.when(leads)
    def _():
        pl.semaphore_wait(barrier, 2 + rows_z - 1)
        for e, a, b in row[1:]:
            say(plane_here, in_plane(0, e, a, b))

    half = width // 2
    lane = lax.broadcasted_iota(jnp.int32, (8, LANES), 1) < half
    sublane = lax.broadcasted_iota(jnp.int32, (8, LANES), 0)
    sign = jnp.where(lax.broadcasted_iota(jnp.int32, (half, width), 1) < half, 1.0, -1.0)

    def products(n, hi):
        for c_to in range(2):
            m = 2 * hi + c_to
            for f in range(RUN):
                at = n * RUN + f
                pair = jnp.concatenate([held[m + 1, at], held[m, at]], 1)
                product = lax.dot_general(
                    held[m + 2, at], pair, (((0,), (0,)), ((), ())), preferred_element_type=F32
                ) * (1.0 / math.sqrt(windows))
                for r in range(ROUNDS):
                    block = product[:, r * width : (r + 1) * width]
                    both = block[:half] * sign + pltpu.roll(block[half:], half, 1)
                    work[pl.ds(((c_to * ROUNDS + r) * RUN + f) * half, half), :] = both
        for shard in range(half // 4):
            real, imag = [], []
            for h in range(2):
                first = work[pl.ds(4 * shard + 2 * h, 8, stride=half), :]
                second = work[pl.ds(4 * shard + 2 * h + 1, 8, stride=half), :]
                real.append(jnp.where(lane, first, pltpu.roll(second, half, 1)))
                imag.append(jnp.where(lane, pltpu.roll(first, half, 1), second))
            for c_to in range(2):
                parts = []
                for lower, upper in (real, imag):
                    if c_to:
                        lower = pltpu.roll(lower, 4, 0)
                    else:
                        upper = pltpu.roll(upper, 4, 0)
                    parts.append(jnp.where(sublane < 4, lower, upper))
                packed[2 * n + hi, shard // 2, c_to, shard % 2] = jnp.concatenate(parts, 0).astype(BF16)

    last = CHUNKS - 1
    relayed = CHUNKS - DIRECT
    far_first = sorted(range(1, rows_z), key=lambda k: -min(k, rows_z - k))

    def z_copy(n, hi, k):
        w = 2 * n + hi
        return pltpu.make_async_remote_copy(
            src_ref=packed.at[w, (z + k) % rows_z],
            dst_ref=relay.at[w, z],
            send_sem=z_send.at[w, k],
            recv_sem=z_recv.at[w, k],
            device_id=device(y, xh, core, (z + k) % rows_z, xl),
            device_id_type=MESH,
        )

    def send_z(n, hi):
        for k in far_first:
            z_copy(n, hi, k).start()
        w = 2 * n + hi
        pltpu.make_async_copy(packed.at[w, z], relay.at[w, z], z_recv.at[w, 0]).start()

    def wait_z(n, hi):
        w = 2 * n + hi
        for k in range(rows_z):
            here = relay.at[w, (z + rows_z - k) % rows_z]
            pltpu.make_async_copy(here, here, z_recv.at[w, k]).wait()

    def row_copy(n, hi, a, b):
        return pltpu.make_async_remote_copy(
            src_ref=relay.at[2 * n + hi, :, (core + b) % 2, (xl + a) % 2],
            dst_ref=landed.at[n, own_source],
            send_sem=row_send.at[n, hi, 2 * a + b],
            recv_sem=row_recv.at[n, 4 * ((xh + hi) % 2) + 2 * a + b],
            device_id=device(y, hi, (core + b) % 2, z, (xl + a) % 2),
            device_id_type=MESH,
        )

    def send_row(n, hi):
        wait_z(n, hi)
        for a, b in ((1, 0), (1, 1), (0, 1)):
            row_copy(n, hi, a, b).start()

        @pl.when(xh != hi)
        def _():
            row_copy(n, hi, 0, 0).start()

        @pl.when(xh == hi)
        def _():
            pltpu.make_async_copy(
                relay.at[2 * n + hi, :, core, xl], landed.at[n, own_source], row_recv.at[n, 0]
            ).start()

    def direct_copy(n, hi, k, a, b):
        to_z, to_core, to_xl = (z + k) % rows_z, (core + b) % 2, (xl + a) % 2
        return pltpu.make_async_remote_copy(
            src_ref=packed.at[2 * n + hi, to_z, to_core, to_xl],
            dst_ref=landed.at[n, own_source, z],
            send_sem=direct_send.at[n - relayed, hi, k, 2 * a + b],
            recv_sem=direct_recv.at[n - relayed],
            device_id=device(y, hi, to_core, to_z, to_xl),
            device_id_type=MESH,
        )

    def send_direct(n, hi):
        for k in far_first:
            for a in range(2):
                for b in range(2):
                    direct_copy(n, hi, k, a, b).start()
        for a, b in ((1, 0), (1, 1), (0, 1)):
            direct_copy(n, hi, 0, a, b).start()

        @pl.when(xh != hi)
        def _():
            direct_copy(n, hi, 0, 0, 0).start()

        @pl.when(xh == hi)
        def _():
            pltpu.make_async_copy(
                packed.at[2 * n + hi, z, core, xl], landed.at[n, own_source, z], direct_recv.at[n - relayed]
            ).start()

    def wait_direct(n):
        pltpu.make_async_copy(landed.at[n], landed.at[n], direct_recv.at[n - relayed]).wait()

    def relays(n, hi):
        return n < relayed or (n == relayed and n < last and hi == 1)

    def send_wave(n, hi):
        if relays(n, hi):
            send_z(n, hi)
        else:
            send_direct(n, hi)

    def wave(n, hi):
        products(n, hi)
        send_wave(n, hi)

    def wait_row(n):
        for k, (e, a, b) in enumerate(row):
            here = landed.at[n, 4 * ((xh + e) % 2) + 2 * ((xl + a) % 2) + (core + b) % 2]
            pltpu.make_async_copy(here, here, row_recv.at[n, k]).wait()

    span = 2 * rows_z * 16

    def sort(n):
        def one(group, carry):
            lo, depth = group // rows_z, group % rows_z
            tiles = [landed[n, 4 * (s // 2) + 2 * lo + s % 2, depth].astype(F32) for s in range(4)]
            at = pl.multiple_of(n * span + group * 16, 16)
            for h in range(2):
                for r in range(ROUNDS):
                    parts = []
                    for c in range(2):
                        value = None
                        for s in range(4):
                            turned = tiles[s][8 * c : 8 * c + 8]
                            amount = 2 * (s - (2 * h + r)) % 8
                            if amount:
                                turned = pltpu.roll(turned, amount, 0)
                            value = turned if value is None else jnp.where(sublane < 2 * s, value, turned)
                        parts.append(value)
                    sorted_[r, pl.ds(at, 16), h * LANES : (h + 1) * LANES] = jnp.concatenate(parts, 0).astype(BF16)
            return carry

        lax.fori_loop(0, 2 * rows_z, one, 0)

    def lag_product(first, stop):
        rows = pl.ds(first * span, (stop - first) * span)

        def one(r, carry):
            value = lax.dot_general(
                sorted_[r, rows, :], table[rows, :], (((0,), (0,)), ((), ())), preferred_element_type=F32
            )
            if stop < CHUNKS:
                total[r] = value
            else:
                out[r, 0] = (total[r] + value).astype(BF16)
            return carry

        lax.fori_loop(0, ROUNDS, one, 0)

    def wait_y(n):
        for p in range(len(pieces[n])):
            y_copy(n, p).wait_recv()

    for p in range(len(pieces[0])):
        forward(0, p)
    products(0, 1)

    @pl.when(jnp.logical_not(leads))
    def _():
        pl.semaphore_wait(plane_here, 1)

    send_wave(0, 1)
    for n in range(last):
        half_way = len(pieces[n + 1]) // 2
        for p in range(half_way):
            forward(n + 1, p)
        wait_y(n)
        wave(n, 0)
        if n + 1 == last:
            for early in range(min(2, relayed)):
                for hi in (1, 0):
                    send_row(early, hi)
        for p in range(half_way, len(pieces[n + 1])):
            forward(n + 1, p)
        wave(n + 1, 1)
    for early in range(2, last):
        for hi in (1, 0):
            if relays(early, hi):
                send_row(early, hi)
    wait_y(last)
    wave(last, 0)
    for n in range(last):
        for hi in range(2):
            @pl.when(xh == hi)
            def _():
                if relays(n, hi):
                    wait_row(n)
                else:
                    wait_direct(n)
        sort(n)
    lag_product(0, last)
    wait_direct(last)
    sort(last)
    lag_product(last, CHUNKS)

    for copy in x_copies:
        copy.wait_send()
    for n in range(CHUNKS):
        for p in range(len(pieces[n])):
            y_copy(n, p).wait_send()
    for n in range(CHUNKS):
        for hi in range(2):
            if relays(n, hi):
                for k in range(1, rows_z):
                    z_copy(n, hi, k).wait_send()
                for a, b in ((1, 0), (1, 1), (0, 1)):
                    row_copy(n, hi, a, b).wait_send()
            else:
                for k in range(rows_z):
                    for a in range(2):
                        for b in range(2):
                            if (k, a, b) != (0, 0, 0):
                                direct_copy(n, hi, k, a, b).wait_send()

            @pl.when(xh != hi)
            def _():
                if relays(n, hi):
                    row_copy(n, hi, 0, 0).wait_send()
                else:
                    direct_copy(n, hi, 0, 0, 0).wait_send()


def in_hbm(array):
    return pltpu.with_memory_space_constraint(array, pltpu.HBM)


def local(rows_y, rows_z, spectra, band_weight):
    _, freqs, windows, width = spectra.shape
    bins = band_weight.shape[0]
    lags = 2 * bins
    pairs = (width // 2) ** 2 // (2 * rows_z)
    held_freqs = CHUNKS * RUN
    rows = CHUNKS * 2 * rows_z * 16
    dma = pltpu.SemaphoreType.DMA
    return pl.pallas_call(
        functools.partial(stack_kernel, rows_y, rows_z),
        name="stack",
        out_shape=jax.ShapeDtypeStruct((ROUNDS, 1, pairs, lags), BF16),
        in_specs=[pl.BlockSpec(memory_space=pltpu.HBM), pl.BlockSpec(memory_space=pltpu.HBM)],
        out_specs=pl.BlockSpec(memory_space=pltpu.VMEM),
        scratch_shapes=[
            pltpu.VMEM((bins // LANES, LANES), F32),
            pltpu.VMEM((6, held_freqs, windows, width), BF16),
            pltpu.VMEM((rows, lags), BF16),
            pltpu.VMEM((bins, LANES), F32),
            pltpu.VMEM((2 * ROUNDS * RUN * width // 2, width), F32),
            pltpu.VMEM((2 * CHUNKS, rows_z, 2, 2, 16, LANES), BF16),
            pltpu.VMEM((2 * CHUNKS, rows_z, 2, 2, 16, LANES), BF16),
            pltpu.VMEM((CHUNKS, 8, rows_z, 16, LANES), BF16),
            pltpu.VMEM((ROUNDS, rows, pairs), BF16),
            pltpu.VMEM((ROUNDS, pairs, lags), F32),
            dma((CHUNKS, 2 * RUN, 4)),
            dma((CHUNKS, 2 * RUN, 4)),
            dma((CHUNKS, 2 * RUN)),
            dma((CHUNKS, 2 * RUN)),
            dma((2 * CHUNKS, rows_z)),
            dma((2 * CHUNKS, rows_z)),
            dma((CHUNKS, 2, 4)),
            dma((CHUNKS, 8)),
            dma((DIRECT, 2, rows_z, 4)),
            dma((DIRECT,)),
            dma,
            pltpu.SemaphoreType.REGULAR,
            pltpu.SemaphoreType.REGULAR,
        ],
        compiler_params=pltpu.CompilerParams(
            collective_id=0, has_side_effects=True, vmem_limit_bytes=48 * 2**20
        ),
    )(in_hbm(spectra), in_hbm(band_weight.reshape(bins // LANES, LANES)))


def solution(mesh):
    rows_y, rows_z = mesh.shape["grp"] // 4, mesh.shape["frq"] // 2
    return jax.shard_map(
        functools.partial(local, rows_y, rows_z),
        mesh=mesh,
        in_specs=(P("grp", "frq", None, None), P()),
        out_specs=P(None, "grp", "frq", None),
        check_vma=False,
    )
```
